256 devices in a mesh: dp: 32 (over x_lo, z, core), mp: 8 (over x_hi, y).
Axes of the slice: x: 4 (x_hi: 2, x_lo: 2; x = x_hi * 2 + x_lo), y: 4, z: 8, core: 2. Of those that a mesh axis runs over, the one named last changes fastest.
Arguments:
- hidden: bfloat16 [4096, 14336], P('dp', 'mp')
- residual: bfloat16 [4096, 4096], P('mp', 'dp'), may hold values from -6 to 6
- down_weight: bfloat16 [14336, 4096], P('mp', 'dp'), may hold values from -6 to 6
- mask: int32 [14336, 4096], P('mp', 'dp'), may hold values 0 or 1
- state: float32 [14336, 4096], P('mp', 'dp'), may hold values from 0.1 to 1
Outputs:
- scores: float32 [14336, 4096], P('mp', 'dp')
- new_weight: bfloat16 [14336, 4096], P('mp', 'dp')
- new_state: float32 [14336, 4096], P('mp', 'dp')
The draws below stay inside these ranges and needn't reach their ends.
All inputs are finite; a program needn't handle non-finite values. No bound on the sum of `mask` on one device may be relied on, other than what follows from the above.
Results may differ from the reference program's by a relative error of at most 0.0029.
Values may be sent and summed in bfloat16 or wider, within the bound.
No kernel may reach another device: no remote copies, remote signals or barrier semaphores. Data moves between devices by JAX's collectives and lax.ppermute only.
A program may use at most 128 MiB of HBM per device.

```python
import math
import jax
import jax.numpy as jnp
from jax import lax

D = 4096
FFW = 14336
TOKENS = 4096


def draw_hidden(key, part):
    key = jax.random.fold_in(key, 11)
    key_col, key_val = jax.random.split(key, 2)
    col_scale = jnp.exp(jax.random.uniform(key_col, (1, FFW), jnp.float32, math.log(0.3), math.log(3.0)))
    position = jnp.arange(TOKENS, dtype=jnp.float32) / TOKENS
    row_scale = jnp.sqrt(0.5 + position)[:, None]
    values = jax.random.normal(key_val, (TOKENS, FFW), jnp.float32) * row_scale
    return (values * col_scale).astype(jnp.bfloat16)


def touch_ends(values, rng, low, high):
    index_at = [jax.random.randint(jax.random.fold_in(rng, axis), (), 0, length) for axis, length in enumerate(values.shape)]
    longest = values.shape.index(max(values.shape))
    beside = index_at[:longest] + [(index_at[longest] + 1) % values.shape[longest]] + index_at[longest + 1:]
    return values.at[tuple(index_at)].set(low).at[tuple(beside)].set(high)


def steps_of(stream_key, dims, cuts, low, largest):
    level = 1.0
    for axis_at, shards_of in cuts:
        heights = jax.random.uniform(jax.random.fold_in(jax.random.fold_in(stream_key, 6), axis_at), (shards_of,), jnp.float32, low / len(cuts), largest / len(cuts))
        level = level * jnp.repeat(jnp.exp(heights), dims[axis_at] // shards_of).reshape((-1,) + (1,) * (len(dims) - 1 - axis_at))
    return level


def noise(key, shape, width, reach, cuts=(), kind=jnp.bfloat16):
    factor_of = steps_of(key, shape, cuts, -0.22, 0.18) if cuts else 1.0
    result = jax.random.normal(key, shape, jnp.float32) * width * factor_of
    return jnp.minimum(jnp.maximum(result, -reach), reach).astype(kind)


def setup_inputs(seed: int = 0) -> dict:
    key_list = jax.random.split(jax.random.key(seed), 6)
    hidden = draw_hidden(jax.random.fold_in(key_list[5], 71), 0)
    residual = noise(key_list[1], (TOKENS, D), 1.0, 6.0, ((0, 8), (1, 32)))
    down_weight = noise(key_list[2], (FFW, D), 1.0, 6.0, ((0, 8), (1, 32)))
    mask = touch_ends((jax.random.randint(key_list[3], (FFW, D), 0, 2) < 1).astype(jnp.int32), jax.random.fold_in(key_list[3], 1), 0, 1)
    state = jnp.clip(jnp.exp(math.log(1.0) - 2.3025851 * jax.random.uniform(key_list[4], (FFW, D), jnp.float32) ** steps_of(key_list[4], (FFW, D), ((0, 8), (1, 32)), -0.2, 0.2)), 0.1, 1.0)
    return dict(hidden=hidden, residual=residual, down_weight=down_weight, mask=mask, state=state)


score_alpha = 0.5
decay_rate = 0.9
step_rate = 0.3
tiny_eps = 1e-08

def reference(hidden, residual, down_weight, mask, state):
    count = hidden.shape[0]
    keep = mask == 1
    pruned_part = jnp.where(keep, jnp.zeros_like(down_weight), -down_weight)
    inv_width = 1.0 / math.sqrt(FFW)
    dense = jnp.dot(hidden, down_weight, preferred_element_type=jnp.float32) * inv_width
    gap = jnp.dot(hidden, pruned_part, preferred_element_type=jnp.float32) * inv_width
    block_out = (residual.astype(jnp.float32) + dense).astype(jnp.bfloat16)
    gap_b = gap.astype(jnp.bfloat16)
    inv_count = 1.0 / math.sqrt(count)
    grad_out = jnp.dot(hidden.T, block_out, preferred_element_type=jnp.float32) * inv_count
    grad_gap = jnp.dot(hidden.T, gap_b, preferred_element_type=jnp.float32) * inv_count
    colsq = lax.optimization_barrier(jnp.sum(jnp.square(hidden.astype(jnp.float32)), axis=0))
    rms = jnp.sqrt(colsq / count + 1e-05)
    weight_f = down_weight.astype(jnp.float32)
    scores = jnp.abs(weight_f) * (score_alpha * jnp.abs(grad_out) + rms[:, None])
    grad_step = jnp.where(keep, grad_gap, jnp.float32(0.0))
    new_state = decay_rate * state + (1.0 - decay_rate) * grad_step * grad_step
    moved = weight_f - step_rate * grad_step / (jnp.sqrt(new_state) + tiny_eps)
    new_weight = jnp.where(keep, moved, jnp.float32(0.0)).astype(jnp.bfloat16)
    return (scores, new_weight, new_state)
```

```python
import math

import jax
import jax.numpy as jnp
from jax import lax
from jax.sharding import PartitionSpec as P

FFW = 14336
TOKENS = 4096

score_alpha = 0.5
decay_rate = 0.9
step_rate = 0.3
tiny_eps = 1e-08

Z = 8
PAIR_CORE = [(i, i ^ 1) for i in range(32)]
PAIR_X = [(i, i ^ 16) for i in range(32)]


def ring_perm():
    out = []
    for i in range(32):
        x, z, c = i // 16, (i // 2) % Z, i % 2
        z = (z + (1 if c == 0 else -1)) % Z
        out.append((i, x * 16 + z * 2 + c))
    return out


RING = ring_perm()


def exchange(value):
    return lax.all_to_all(value, "mp", 0, 0, tiled=True)


def body(hidden, residual, down_weight, mask, state):
    f32, bf16 = jnp.float32, jnp.bfloat16
    dp = lax.axis_index("dp")
    mp = lax.axis_index("mp")
    x, z, c = dp >> 4, (dp >> 1) & 7, dp & 1
    rows, cols = hidden.shape[0], down_weight.shape[1]
    keep = mask == 1
    inv_width = 1.0 / math.sqrt(FFW)
    inv_count = 1.0 / math.sqrt(TOKENS)

    sibling = lax.ppermute(hidden, "dp", PAIR_CORE)
    first = jnp.concatenate([hidden, sibling], axis=0)
    r1 = lax.ppermute(first, "dp", RING)
    s1 = lax.ppermute(r1, "dp", PAIR_CORE)
    r2 = lax.ppermute(r1, "dp", RING)
    s2 = lax.ppermute(r2, "dp", PAIR_CORE)
    r3 = lax.ppermute(r2, "dp", RING)
    s3 = lax.ppermute(r3, "dp", PAIR_CORE)
    r4 = lax.ppermute(r3[:rows], "dp", RING)
    s4 = lax.ppermute(r4, "dp", PAIR_CORE)

    pruned_part = jnp.where(keep, jnp.zeros_like(down_weight), -down_weight)
    paired = jnp.concatenate([down_weight, pruned_part], axis=1)
    paired_x = lax.ppermute(paired, "dp", PAIR_X)
    residual_x = lax.ppermute(residual, "dp", PAIR_X)
    weights = jnp.concatenate([paired, paired_x], axis=1)
    zero = jnp.zeros((rows, cols), f32)

    def residual_rows(step, core):
        at = (z + step) & 7
        here = mp == (x << 2) + (at >> 1)
        start = ((at & 1) << 8) + (core << 7)
        own = lax.dynamic_slice(residual, (start, 0), (rows, cols)).astype(f32)
        other = lax.dynamic_slice(residual_x, (start, 0), (rows, cols)).astype(f32)
        both = jnp.concatenate([own, zero, other, zero], axis=1)
        return jnp.where(here, both, 0.0)

    back = jnp.where(c == 0, -1, 1)
    parts = [
        (first, [(0, c), (0, 1 - c)]),
        (r1, [(back, c), (back, 1 - c)]),
        (s1, [(-back, 1 - c), (-back, c)]),
        (r2, [(2 * back, c), (2 * back, 1 - c)]),
        (s2, [(-2 * back, 1 - c), (-2 * back, c)]),
        (r3, [(3 * back, c), (3 * back, 1 - c)]),
        (s3, [(-3 * back, 1 - c), (-3 * back, c)]),
        (r4, [(4, c)]),
        (s4, [(4, 1 - c)]),
    ]
    groups = [parts[:3], parts[3:5], parts[5:]]

    colsq = 0.0
    grads = 0.0
    blocks = []
    for group in groups:
        tokens = jnp.concatenate([p for p, _ in group], axis=0)
        start = jnp.concatenate(
            [residual_rows(k, q) for _, where in group for k, q in where], axis=0
        )
        value = jnp.dot(tokens, weights, preferred_element_type=f32) * inv_width + start
        sent = exchange(value.astype(bf16))
        count = tokens.shape[0] // 8
        summed = jnp.sum(sent.reshape(8, count, 4 * cols).astype(f32), axis=0)
        target = summed.astype(bf16)
        spread = jnp.broadcast_to(target[None], (8, count, 4 * cols)).reshape(8 * count, 4 * cols)
        blocks.append((tokens, exchange(spread)))
        colsq = colsq + jnp.sum(jnp.square(tokens.astype(f32)), axis=0)

    for tokens, targets in blocks:
        grads = grads + lax.dot_general(
            tokens, targets, (((0,), (0,)), ((), ())), preferred_element_type=f32
        )
    grads = grads * inv_count
    colsq = colsq + lax.ppermute(colsq, "dp", PAIR_X)
    arrived = lax.ppermute(grads[:, 2 * cols :].astype(bf16), "dp", PAIR_X)
    grads = grads[:, : 2 * cols] + arrived.astype(f32)

    grad_out = grads[:, :cols]
    grad_step = jnp.where(keep, grads[:, cols:], jnp.float32(0.0))
    rms = jnp.sqrt(colsq / TOKENS + 1e-05)
    weight_f = down_weight.astype(f32)
    scores = jnp.abs(weight_f) * (score_alpha * jnp.abs(grad_out) + rms[:, None])
    new_state = decay_rate * state + (1.0 - decay_rate) * grad_step * grad_step
    moved = weight_f - step_rate * grad_step / (jnp.sqrt(new_state) + tiny_eps)
    new_weight = jnp.where(keep, moved, jnp.float32(0.0)).astype(bf16)
    return (scores, new_weight, new_state)


def solution(mesh):
    return jax.shard_map(
        body,
        mesh=mesh,
        in_specs=(P("dp", "mp"), P("mp", "dp"), P("mp", "dp"), P("mp", "dp"), P("mp", "dp")),
        out_specs=(P("mp", "dp"), P("mp", "dp"), P("mp", "dp")),
        check_vma=False,
    )
```

```python
import functools
import math

import jax
import jax.numpy as jnp
from jax import lax
from jax.experimental import pallas as pl
from jax.experimental.pallas import tpu as pltpu
from jax.sharding import PartitionSpec as P

FFW = 14336
TOKENS = 4096

score_alpha = 0.5
decay_rate = 0.9
step_rate = 0.3
tiny_eps = 1e-08

Z = 8
MP = 8
PAIR_CORE = [(i, i ^ 1) for i in range(32)]
PAIR_X = [(i, i ^ 16) for i in range(32)]
OFFSETS = [(0, 1), (0, 3), (1, 0), (0, 2), (1, 1), (1, 3), (1, 2)]
VMEM_LIMIT = 24 * 1024 * 1024

f32, bf16 = jnp.float32, jnp.bfloat16


def ring_perm():
    out = []
    for i in range(32):
        x, z, c = i // 16, (i // 2) % Z, i % 2
        z = (z + (1 if c == 0 else -1)) % Z
        out.append((i, x * 16 + z * 2 + c))
    return out


RING = ring_perm()


def mp_perm(dx, dy):
    return [(j, ((j // 4) ^ dx) * 4 + (j % 4 + dy) % 4) for j in range(MP)]


def vmem_call(kernel, out_shape, scratch, flops, n_after, name, ids, *args):
    vmem = pl.BlockSpec(memory_space=pltpu.VMEM)
    specs = [pl.BlockSpec(memory_space=pltpu.SMEM)]
    specs += [vmem] * (len(args) - n_after)
    specs += [pl.BlockSpec(memory_space=pl.ANY)] * n_after
    moved = sum(a.size * a.dtype.itemsize for a in args)
    return pl.pallas_call(
        kernel,
        out_shape=out_shape,
        in_specs=specs,
        out_specs=jax.tree.map(lambda _: vmem, out_shape),
        scratch_shapes=scratch,
        compiler_params=pltpu.CompilerParams(vmem_limit_bytes=VMEM_LIMIT),
        cost_estimate=pl.CostEstimate(flops=flops, bytes_accessed=moved, transcendentals=0),
        name=name,
    )(ids, *args)


def peer(mp, offset, sign):
    dx, dy = offset
    return (((mp >> 2) ^ dx) << 2) + ((mp + sign * dy) & 3)


def forward_kernel(places, n, rows, scale, ids, *refs):
    blocks = refs[:n]
    w_ref, p_ref, wx_ref, px_ref, res_ref, resx_ref = refs[n : n + 6]
    outs, sq_ref, wide, held = refs[-MP - 3 : -3], refs[-3], refs[-2], refs[-1]
    dp, mp = ids[0], ids[1]
    x, z, c = dp >> 4, (dp >> 1) & 7, dp & 1
    back = 2 * c - 1
    cols = res_ref.shape[1]
    for k, ref in enumerate((w_ref, p_ref, wx_ref, px_ref)):
        wide[:, k * cols : (k + 1) * cols] = ref[...]
    total = jnp.zeros((8, w_ref.shape[0]), f32)
    for b in range(0, n, 2):
        tokens = jnp.concatenate([blocks[b][...], blocks[b + 1][...]], axis=0)
        for side, res in enumerate((res_ref, resx_ref)):
            left = side * 2 * cols
            weights = wide[:, left : left + 2 * cols]
            value = jnp.dot(tokens, weights, preferred_element_type=f32) * scale
            for half in range(2):
                step, same = places[b + half]
                at = (z + step * back) & 7
                core = c if same else 1 - c
                here = mp == (x << 2) + (at >> 1)
                start = pl.multiple_of(((at & 1) << 8) + (core << 7), rows)
                extra = jnp.where(here, res[pl.ds(start, rows), :].astype(f32), 0.0)
                part = value[half * rows : (half + 1) * rows]
                to = pl.ds((b + half) * rows, rows)
                held[to, left : left + cols] = (part[:, :cols] + extra).astype(bf16)
                held[to, left + cols : left + 2 * cols] = part[:, cols:].astype(bf16)
        squares = jnp.square(tokens.astype(f32))
        total = total + jnp.sum(squares.reshape(2 * rows // 8, 8, squares.shape[1]), axis=0)
    sq_ref[...] = jnp.sum(total, axis=0, keepdims=True)
    count = n * rows // MP
    for out, to in zip(outs, [mp] + [peer(mp, o, 1) for o in OFFSETS]):
        out[...] = held[pl.ds(pl.multiple_of(to * count, 32), count), :]


def forward(ids, blocks, places, weights, residuals, after=()):
    n, (rows, width), cols = len(blocks), blocks[0].shape, residuals[0].shape[1]
    piece = jax.ShapeDtypeStruct((n * rows // MP, 4 * cols), bf16)
    out = vmem_call(
        functools.partial(forward_kernel, places, n, rows, 1.0 / math.sqrt(FFW)),
        [piece] * MP + [jax.ShapeDtypeStruct((1, width), f32)],
        [pltpu.VMEM((width, 4 * cols), bf16), pltpu.VMEM((n * rows, 4 * cols), bf16)],
        2 * n * rows * width * 4 * cols,
        len(after),
        "forward",
        ids,
        *blocks,
        *weights,
        *residuals,
        *after,
    )
    return out[:MP], out[MP]


def merge_kernel(ids, *refs):
    o_ref = refs[-1]
    count = o_ref.shape[0]
    for r in range(0, count, 32):
        at = pl.ds(r, 32)
        total = refs[0][at, :].astype(f32)
        for piece in refs[1:MP]:
            total = total + piece[at, :].astype(f32)
        o_ref[at, :] = total.astype(bf16)


def merge(ids, pieces, after=()):
    shape = pieces[0].shape
    return vmem_call(
        merge_kernel,
        jax.ShapeDtypeStruct(shape, bf16),
        [],
        MP * pieces[0].size,
        len(after),
        "merge",
        ids,
        *pieces,
        *after,
    )


def backward_kernel(n, scale, n_init, parts, ids, *refs):
    blocks, pieces, inits = refs[:n], refs[n : n + MP], refs[n + MP : n + MP + n_init]
    outs, held = refs[-1 - len(parts) : -1], refs[-1]
    mp = ids[1]
    count = pieces[0].shape[0]
    for piece, source in zip(pieces, [mp] + [peer(mp, o, -1) for o in OFFSETS]):
        held[pl.ds(pl.multiple_of(source * count, 32), count), :] = piece[...]
    width = blocks[0].shape[1]
    for at in range(0, width, 256):
        tokens = jnp.concatenate([block[:, at : at + 256] for block in blocks], axis=0)
        for k, (left, right) in enumerate(parts):
            value = lax.dot_general(
                tokens,
                held[:, left:right],
                (((0,), (0,)), ((), ())),
                preferred_element_type=f32,
            )
            value = value * scale
            if n_init:
                value = value + inits[k][at : at + 256, :]
            outs[k][at : at + 256, :] = value.astype(outs[k].dtype)


def backward(ids, blocks, pieces, inits, parts, dtype):
    n, (rows, width) = len(blocks), blocks[0].shape
    return vmem_call(
        functools.partial(backward_kernel, n, 1.0 / math.sqrt(TOKENS), len(inits), parts),
        [jax.ShapeDtypeStruct((width, r - l), dtype) for l, r in parts],
        [pltpu.VMEM((n * rows, pieces[0].shape[1]), bf16)],
        2 * n * rows * width * sum(r - l for l, r in parts),
        0,
        "backward",
        ids,
        *blocks,
        *pieces,
        *inits,
    )


def gate_kernel(*refs):
    pass


def gate(value, *after):
    hbm = pl.BlockSpec(memory_space=pl.ANY)
    return pl.pallas_call(
        gate_kernel,
        out_shape=jax.ShapeDtypeStruct(value.shape, value.dtype),
        in_specs=[hbm] * (1 + len(after)),
        out_specs=hbm,
        input_output_aliases={0: 0},
        compiler_params=pltpu.CompilerParams(vmem_limit_bytes=1024 * 1024),
        cost_estimate=pl.CostEstimate(flops=0, bytes_accessed=0, transcendentals=0),
        name="gate",
    )(value, *after)


def body(hidden, residual, down_weight, mask, state):
    ids = jnp.stack([lax.axis_index("dp"), lax.axis_index("mp")]).astype(jnp.int32)
    cols = down_weight.shape[1]
    keep = mask == 1

    def ring(value):
        return lax.ppermute(value, "dp", RING)

    def swap(value):
        return lax.ppermute(value, "dp", PAIR_CORE)

    def across(value):
        return lax.ppermute(value, "dp", PAIR_X)

    def around(pieces):
        return [lax.ppermute(v, "mp", mp_perm(*o)) for v, o in zip(pieces, OFFSETS)]

    sib = swap(hidden)
    a1 = ring(hidden)
    b1 = ring(sib)
    weight_x = across(down_weight)
    residual_x = across(residual)
    pruned = jnp.where(keep, jnp.zeros_like(down_weight), -down_weight)
    pruned_x = across(pruned)
    a1 = gate(a1, pruned)
    a2 = ring(a1)
    sa1 = swap(a1)
    b2 = ring(b1)
    sb1 = swap(b1)
    a2 = gate(a2, sa1, sb1, weight_x, residual_x)
    a3 = ring(a2)
    sa2 = swap(a2)
    b3 = ring(b2)
    sb2 = swap(b2)
    a4 = ring(a3)
    sa3 = swap(a3)
    sb3 = swap(b3)

    weights = (down_weight, pruned, weight_x, pruned_x)
    residuals = (residual, residual_x)
    early_blocks = [hidden, sib, a1, b1, sa1, sb1, a2, b2, sa2, sb2]
    early_places = [(0, 1), (0, 0), (1, 1), (1, 0), (-1, 0), (-1, 1)]
    early_places += [(2, 1), (2, 0), (-2, 0), (-2, 1)]
    value0, squares0 = forward(ids, early_blocks, early_places, weights, residuals)
    a4 = gate(a4, squares0)
    sa4 = swap(a4)
    got0 = around(value0[1:])
    late_blocks = [a3, b3, sa3, sb3, a4, sa4]
    late_places = [(3, 1), (3, 0), (-3, 0), (-3, 1), (4, 1), (4, 0)]
    value1, squares1 = forward(ids, late_blocks, late_places, weights, residuals, got0[:2])
    got1 = around(value1[1:])
    colsq = squares0 + squares1
    colsq = colsq + across(colsq)

    mine0 = merge(ids, [value0[0]] + got0, [squares1])
    target0 = [mine0] + around([mine0] * (MP - 1))
    mine1 = merge(ids, [value1[0]] + got1)
    target1 = [mine1] + around([mine1] * (MP - 1))

    own, other = (0, 2 * cols), (2 * cols, 4 * cols)
    early_own, early_other = backward(ids, early_blocks, target0, [], [own, other], f32)
    (sent,) = backward(ids, late_blocks, target1, [early_other], [other], bf16)
    arrived = across(sent)
    (grads,) = backward(ids, late_blocks, target1, [early_own], [own], f32)
    grads = grads + arrived.astype(f32)

    grad_out = grads[:, :cols]
    grad_step = jnp.where(keep, grads[:, cols:], jnp.float32(0.0))
    rms = jnp.sqrt(colsq.reshape(-1) / TOKENS + 1e-05)
    weight_f = down_weight.astype(f32)
    scores = jnp.abs(weight_f) * (score_alpha * jnp.abs(grad_out) + rms[:, None])
    new_state = decay_rate * state + (1.0 - decay_rate) * grad_step * grad_step
    moved = weight_f - step_rate * grad_step / (jnp.sqrt(new_state) + tiny_eps)
    new_weight = jnp.where(keep, moved, jnp.float32(0.0)).astype(bf16)
    return (scores, new_weight, new_state)


def solution(mesh):
    return jax.shard_map(
        body,
        mesh=mesh,
        in_specs=(P("dp", "mp"), P("mp", "dp"), P("mp", "dp"), P("mp", "dp"), P("mp", "dp")),
        out_specs=(P("mp", "dp"), P("mp", "dp"), P("mp", "dp")),
        check_vma=False,
    )
```

```python
import functools
import math

import jax
import jax.numpy as jnp
from jax import lax
from jax.experimental import pallas as pl
from jax.experimental.pallas import tpu as pltpu
from jax.sharding import PartitionSpec as P

FFW = 14336
TOKENS = 4096

score_alpha = 0.5
decay_rate = 0.9
step_rate = 0.3
tiny_eps = 1e-08

Z = 8
MP = 8
PAIR_CORE = [(i, i ^ 1) for i in range(32)]
PAIR_X = [(i, i ^ 16) for i in range(32)]
VMEM_LIMIT = 16 * 1024 * 1024

f32, bf16 = jnp.float32, jnp.bfloat16


def ring_perm():
    out = []
    for i in range(32):
        x, z, c = i // 16, (i // 2) % Z, i % 2
        z = (z + (1 if c == 0 else -1)) % Z
        out.append((i, x * 16 + z * 2 + c))
    return out


RING = ring_perm()


def y_perm(dy):
    return [(j, (j // 4) * 4 + (j % 4 + dy) % 4) for j in range(MP)]


PAIR_X_HI = [(j, j ^ 4) for j in range(MP)]
AHEAD = (1, 3, 2)


def place():
    dp, mp = lax.axis_index("dp"), lax.axis_index("mp")
    return dp >> 4, (dp >> 1) & 7, dp & 1, mp >> 2, mp & 3


def rows_at(block, count):
    return pl.ds(pl.multiple_of(block * count, 32), count)


def vmem_call(kernel, out_shape, scratch, flops, n_after, name, *args):
    vmem = pl.BlockSpec(memory_space=pltpu.VMEM)
    specs = [vmem] * (len(args) - n_after)
    specs += [pl.BlockSpec(memory_space=pl.ANY)] * n_after
    moved = sum(a.size * a.dtype.itemsize for a in args)
    return pl.pallas_call(
        kernel,
        out_shape=out_shape,
        in_specs=specs,
        out_specs=jax.tree.map(lambda _: vmem, out_shape),
        scratch_shapes=scratch,
        compiler_params=pltpu.CompilerParams(vmem_limit_bytes=VMEM_LIMIT),
        cost_estimate=pl.CostEstimate(flops=0, bytes_accessed=0, transcendentals=0),
        name=name,
    )(*args)


def stack_kernel(n, *refs):
    rows = refs[0].shape[0]
    for k in range(n):
        refs[-1][k * rows : (k + 1) * rows, :] = refs[k][...]


def stack(blocks, after=()):
    rows, width = blocks[0].shape
    return vmem_call(
        functools.partial(stack_kernel, len(blocks)),
        jax.ShapeDtypeStruct((len(blocks) * rows, width), bf16),
        [],
        0,
        len(after),
        "stack",
        *blocks,
        *after,
    )


ROWS = 128


def forward_kernel(units, places, scale, more, *refs):
    blocks = refs[: sum(units)]
    packs, residuals = refs[sum(units) :][:4], refs[sum(units) + 4 :][:2]
    mine, ahead, sq_ref, wide, held = refs[-7], refs[-6:-3], refs[-3], refs[-2], refs[-1]
    x, z, c, x_hi, y = place()
    back = 2 * c - 1
    width, cols = blocks[0].shape[1], packs[0].shape[1]
    for k, ref in enumerate(packs):
        wide[:, k * cols : (k + 1) * cols] = ref[...]
    total = jnp.zeros((8, width), f32)
    first, row = 0, 0
    for unit in units:
        group = [block[...] for block in blocks[first : first + unit]]
        tokens = jnp.concatenate(group, axis=0) if unit > 1 else group[0]
        first += unit
        for side, ref in enumerate(residuals):
            left = side * 2 * cols
            weights = wide[:, left : left + 2 * cols]
            value = jnp.dot(tokens, weights, preferred_element_type=f32) * scale
            for k in range(tokens.shape[0] // ROWS):
                step, same = places[row // ROWS + k]
                at = (z + step * back) & 7
                core = c if same else 1 - c
                here = (x_hi << 2) + y == (x << 2) + (at >> 1)
                start = pl.multiple_of(((at & 1) << 8) + (core << 7), ROWS)
                extra = jnp.where(here, ref[pl.ds(start, ROWS), :].astype(f32), 0.0)
                part = value[k * ROWS : (k + 1) * ROWS]
                to = pl.ds(row + k * ROWS, ROWS)
                held[to, left : left + cols] = part[:, :cols] + extra
                held[to, left + cols : left + 2 * cols] = part[:, cols:]
        squares = jnp.square(tokens.astype(f32))
        total = total + jnp.sum(squares.reshape(-1, 8, width), axis=0)
        row += tokens.shape[0]
    total = jnp.sum(total, axis=0, keepdims=True)
    sq_ref[...] = total + refs[sum(units) + 6][...] if more else total
    quarter = held.shape[0] // 4
    mine[...] = held[rows_at(y, quarter), :]
    for out, dy in zip(ahead, AHEAD):
        out[...] = held[rows_at((y + dy) & 3, quarter), :].astype(bf16)


def forward(units, places, packs, squares=(), after=()):
    blocks = [block for unit in units for block in unit]
    rows = sum(block.shape[0] for block in blocks)
    width, cols = blocks[0].shape[1], packs[0].shape[1]
    piece = (rows // 4, 4 * cols)
    out = vmem_call(
        functools.partial(
            forward_kernel,
            [len(unit) for unit in units],
            places,
            1.0 / math.sqrt(FFW),
            len(squares),
        ),
        [jax.ShapeDtypeStruct(piece, f32)]
        + [jax.ShapeDtypeStruct(piece, bf16)] * 3
        + [jax.ShapeDtypeStruct((1, width), f32)],
        [pltpu.VMEM((width, 4 * cols), bf16), pltpu.VMEM((rows, 4 * cols), f32)],
        2 * rows * width * 4 * cols,
        len(after),
        "forward",
        *blocks,
        *packs,
        *squares,
        *after,
    )
    return out[0], out[1:4], out[4]


def merge_y_kernel(*refs):
    pieces, (keep, send) = refs[:4], refs[-2:]
    x_hi = place()[3]
    count = keep.shape[0]
    for out, half in ((send, 1 - x_hi), (keep, x_hi)):
        for r in range(0, count, 32):
            at = pl.ds(pl.multiple_of(half * count + r, 32), 32)
            total = pieces[0][at, :]
            for piece in pieces[1:]:
                total = total + piece[at, :].astype(f32)
            out[r : r + 32, :] = total.astype(out.dtype)


def merge_y(mine, got, after=()):
    rows, width = mine.shape
    return vmem_call(
        merge_y_kernel,
        [jax.ShapeDtypeStruct((rows // 2, width), t) for t in (f32, bf16)],
        [],
        4 * mine.size,
        len(after),
        "merge_y",
        mine,
        *got,
        *after,
    )


def merge_x_kernel(keep, got, *refs):
    refs[-1][...] = (keep[...] + got[...].astype(f32)).astype(bf16)


def merge_x(keep, got, after=()):
    return vmem_call(
        merge_x_kernel,
        jax.ShapeDtypeStruct(keep.shape, bf16),
        [],
        keep.size,
        len(after),
        "merge_x",
        keep,
        got,
        *after,
    )


def pair_kernel(n, mine, got, *refs):
    outs = refs[-n:]
    x_hi = place()[3]
    count, part = mine.shape[0], outs[0].shape[1]
    for piece, at in ((mine, x_hi), (got, 1 - x_hi)):
        for k, out in enumerate(outs):
            out[rows_at(at, count), :] = piece[:, k * part : (k + 1) * part]


def pair(mine, got, parts, after=()):
    count, width = mine.shape
    return vmem_call(
        functools.partial(pair_kernel, parts),
        [jax.ShapeDtypeStruct((2 * count, width // parts), bf16)] * parts,
        [],
        2 * mine.size,
        len(after),
        "pair",
        mine,
        got,
        *after,
    )


def backward_kernel(n, scale, left, *refs):
    blocks, targets, o_ref, held = refs[:n], refs[n : n + 4], refs[-2], refs[-1]
    y = place()[4]
    width, cols = blocks[0].shape[1], held.shape[1]
    for ref, dy in zip(targets, (0,) + AHEAD):
        held[rows_at((y - dy) & 3, ref.shape[0]), :] = ref[...]
    for at in range(0, width, 256):
        tokens = jnp.concatenate([block[:, at : at + 256] for block in blocks], axis=0)
        value = lax.dot_general(
            tokens, held[...], (((0,), (0,)), ((), ())), preferred_element_type=f32
        )
        value = value * scale
        if left is not None:
            value = value + refs[n + 4][at : at + 256, left : left + cols]
        o_ref[at : at + 256, :] = value.astype(o_ref.dtype)


def backward(blocks, targets, dtype, init=(), left=None):
    n, width, cols = len(blocks), blocks[0].shape[1], targets[0].shape[1]
    rows = sum(block.shape[0] for block in blocks)
    return vmem_call(
        functools.partial(backward_kernel, n, 1.0 / math.sqrt(TOKENS), left),
        jax.ShapeDtypeStruct((width, cols), dtype),
        [pltpu.VMEM((rows, cols), bf16)],
        2 * rows * width * cols,
        0,
        "backward",
        *blocks,
        *targets,
        *init,
    )


def gate_kernel(*refs):
    pass


def gate(value, *after):
    hbm = pl.BlockSpec(memory_space=pl.ANY)
    return pl.pallas_call(
        gate_kernel,
        out_shape=jax.ShapeDtypeStruct(value.shape, value.dtype),
        in_specs=[hbm] * (1 + len(after)),
        out_specs=hbm,
        input_output_aliases={0: 0},
        compiler_params=pltpu.CompilerParams(vmem_limit_bytes=1024 * 1024),
        cost_estimate=pl.CostEstimate(flops=0, bytes_accessed=0, transcendentals=0),
        name="gate",
    )(value, *after)


def body(hidden, residual, down_weight, mask, state):
    cols = down_weight.shape[1]
    keep = mask == 1

    def ring(value):
        return lax.ppermute(value, "dp", RING)

    def swap(value):
        return lax.ppermute(value, "dp", PAIR_CORE)

    def across(value):
        return lax.ppermute(value, "dp", PAIR_X)

    def around(pieces):
        return [lax.ppermute(v, "mp", y_perm(dy)) for v, dy in zip(pieces, AHEAD)]

    def over(value):
        return lax.ppermute(value, "mp", PAIR_X_HI)

    sib = swap(hidden)
    a1 = ring(hidden)
    b1 = ring(sib)
    weight_x = across(down_weight)
    pruned = jnp.where(keep, jnp.zeros_like(down_weight), -down_weight)
    pruned_x = across(pruned)
    residual_x = across(residual)
    a1 = gate(a1, pruned)
    a2 = ring(a1)
    sa1 = swap(a1)
    b2 = ring(b1)
    sb1 = swap(b1)
    a2 = gate(a2, sa1, sb1, weight_x, pruned_x)
    a3 = ring(a2)
    sa2 = swap(a2)
    b2 = gate(b2, residual_x)
    b3 = ring(b2)

    packs = (down_weight, pruned, weight_x, pruned_x, residual, residual_x)
    early = [[hidden, sib], [a1, b1], [sa1, sb1], [a2, sa2]]
    places = [(0, 1), (0, 0), (1, 1), (1, 0), (-1, 0), (-1, 1), (2, 1), (-2, 0)]
    mine0, ahead0, squares0 = forward(early, places, packs)
    got0 = around(ahead0)
    a3 = gate(a3, squares0)
    a4 = ring(a3)
    keep0, send0 = merge_y(mine0, got0)
    b3 = gate(b3, keep0)
    s4 = stack([b2, a3, b3, a4])
    t4 = swap(s4)
    sent0 = over(send0)
    late = [s4, t4]
    places = [(2, 0), (3, 1), (3, 0), (4, 1), (-2, 1), (-3, 0), (-3, 1), (4, 0)]
    mine1, ahead1, squares = forward([[s4], [t4]], places, packs, [squares0], [sent0])
    got1 = around(ahead1)
    squares_x = across(squares)

    early = [block for unit in early for block in unit]
    sum0 = merge_x(keep0, sent0)
    keep1, send1 = merge_y(mine1, got1, [sum0])
    (both0,) = pair(sum0, over(sum0), 1, [keep1])
    sum1 = merge_x(keep1, over(send1), [both0])
    init = backward(early, [both0] + around([both0] * 3), f32)
    own1, other1 = pair(sum1, over(sum1), 2, [init])
    other1 = [other1] + around([other1] * 3)
    own1 = [own1] + around([own1] * 3)
    arrived = across(backward(late, other1, bf16, [init], 2 * cols))
    grads = backward(late, own1, f32, [init], 0)
    colsq = squares + squares_x
    grads = grads + arrived.astype(f32)

    grad_out = grads[:, :cols]
    grad_step = jnp.where(keep, grads[:, cols:], jnp.float32(0.0))
    rms = jnp.sqrt(colsq.reshape(-1) / TOKENS + 1e-05)
    weight_f = down_weight.astype(f32)
    scores = jnp.abs(weight_f) * (score_alpha * jnp.abs(grad_out) + rms[:, None])
    new_state = decay_rate * state + (1.0 - decay_rate) * grad_step * grad_step
    moved = weight_f - step_rate * grad_step / (jnp.sqrt(new_state) + tiny_eps)
    new_weight = jnp.where(keep, moved, jnp.float32(0.0)).astype(bf16)
    return (scores, new_weight, new_state)


def solution(mesh):
    return jax.shard_map(
        body,
        mesh=mesh,
        in_specs=(P("dp", "mp"), P("mp", "dp"), P("mp", "dp"), P("mp", "dp"), P("mp", "dp")),
        out_specs=(P("mp", "dp"), P("mp", "dp"), P("mp", "dp")),
        check_vma=False,
    )
```

```python
import functools
import math

import jax
import jax.numpy as jnp
from jax import lax
from jax.experimental import pallas as pl
from jax.experimental.pallas import tpu as pltpu
from jax.sharding import PartitionSpec as P

FFW = 14336
TOKENS = 4096

score_alpha = 0.5
decay_rate = 0.9
step_rate = 0.3
tiny_eps = 1e-08

Z = 8
MP = 8
PAIR_CORE = [(i, i ^ 1) for i in range(32)]
PAIR_X = [(i, i ^ 16) for i in range(32)]
VMEM_LIMIT = 16 * 1024 * 1024

f32, bf16 = jnp.float32, jnp.bfloat16


def ring_perm():
    out = []
    for i in range(32):
        x, z, c = i // 16, (i // 2) % Z, i % 2
        z = (z + (1 if c == 0 else -1)) % Z
        out.append((i, x * 16 + z * 2 + c))
    return out


RING = ring_perm()


def y_perm(dy):
    return [(j, (j // 4) * 4 + (j % 4 + dy) % 4) for j in range(MP)]


PAIR_X_HI = [(j, j ^ 4) for j in range(MP)]
AHEAD = (1, 3, 2)


def place():
    dp, mp = lax.axis_index("dp"), lax.axis_index("mp")
    return dp >> 4, (dp >> 1) & 7, dp & 1, mp >> 2, mp & 3


def rows_at(block, count):
    return pl.ds(pl.multiple_of(block * count, 32), count)


def vmem_call(kernel, out_shape, scratch, flops, n_after, name, *args):
    vmem = pl.BlockSpec(memory_space=pltpu.VMEM)
    specs = [vmem] * (len(args) - n_after)
    specs += [pl.BlockSpec(memory_space=pl.ANY)] * n_after
    moved = sum(a.size * a.dtype.itemsize for a in args)
    return pl.pallas_call(
        kernel,
        out_shape=out_shape,
        in_specs=specs,
        out_specs=jax.tree.map(lambda _: vmem, out_shape),
        scratch_shapes=scratch,
        compiler_params=pltpu.CompilerParams(vmem_limit_bytes=VMEM_LIMIT),
        cost_estimate=pl.CostEstimate(flops=0, bytes_accessed=0, transcendentals=0),
        name=name,
    )(*args)


def stack_kernel(n, *refs):
    rows = refs[0].shape[0]
    for k in range(n):
        refs[-1][k * rows : (k + 1) * rows, :] = refs[k][...]


def stack(blocks, after=()):
    rows, width = blocks[0].shape
    return vmem_call(
        functools.partial(stack_kernel, len(blocks)),
        jax.ShapeDtypeStruct((len(blocks) * rows, width), bf16),
        [],
        0,
        len(after),
        "stack",
        *blocks,
        *after,
    )


ROWS = 128


def forward_kernel(units, places, scale, more, sides, *refs):
    blocks = refs[: sum(units)]
    packs, residuals = refs[sum(units) :][:4], refs[sum(units) + 4 :][:2]
    mine, ahead = refs[-4 - 3 * sides], refs[-3 - 3 * sides : -3]
    sq_ref, wide, held = refs[-3:]
    x, z, c, x_hi, y = place()
    back = 2 * c - 1
    width, cols = blocks[0].shape[1], packs[0].shape[1]
    for k, ref in enumerate(packs):
        wide[:, k * cols : (k + 1) * cols] = ref[...]
    total = jnp.zeros((8, width), f32)
    first, row = 0, 0
    for unit in units:
        group = [block[...] for block in blocks[first : first + unit]]
        tokens = jnp.concatenate(group, axis=0) if unit > 1 else group[0]
        first += unit
        for side, ref in enumerate(residuals):
            left = side * 2 * cols
            weights = wide[:, left : left + 2 * cols]
            value = jnp.dot(tokens, weights, preferred_element_type=f32) * scale
            for k in range(tokens.shape[0] // ROWS):
                step, same = places[row // ROWS + k]
                at = (z + step * back) & 7
                core = c if same else 1 - c
                here = (x_hi << 2) + y == (x << 2) + (at >> 1)
                start = pl.multiple_of(((at & 1) << 8) + (core << 7), ROWS)
                extra = jnp.where(here, ref[pl.ds(start, ROWS), :].astype(f32), 0.0)
                part = value[k * ROWS : (k + 1) * ROWS]
                to = pl.ds(row + k * ROWS, ROWS)
                held[to, left : left + cols] = part[:, :cols] + extra
                held[to, left + cols : left + 2 * cols] = part[:, cols:]
        squares = jnp.square(tokens.astype(f32))
        total = total + jnp.sum(squares.reshape(-1, 8, width), axis=0)
        row += tokens.shape[0]
    total = jnp.sum(total, axis=0, keepdims=True)
    sq_ref[...] = total + refs[sum(units) + 6][...] if more else total
    quarter = held.shape[0] // 4
    mine[...] = held[rows_at(y, quarter), :]
    part = held.shape[1] // sides
    for k, out in enumerate(ahead):
        at = rows_at((y + AHEAD[k % 3]) & 3, quarter)
        left = (k // 3) * part
        out[...] = held[at, left : left + part].astype(bf16)


def forward(units, places, packs, sides, squares=(), after=()):
    blocks = [block for unit in units for block in unit]
    rows = sum(block.shape[0] for block in blocks)
    width, cols = blocks[0].shape[1], packs[0].shape[1]
    piece = (rows // 4, 4 * cols)
    out = vmem_call(
        functools.partial(
            forward_kernel,
            [len(unit) for unit in units],
            places,
            1.0 / math.sqrt(FFW),
            len(squares),
            sides,
        ),
        [jax.ShapeDtypeStruct(piece, f32)]
        + [jax.ShapeDtypeStruct((rows // 4, 4 * cols // sides), bf16)] * (3 * sides)
        + [jax.ShapeDtypeStruct((1, width), f32)],
        [pltpu.VMEM((width, 4 * cols), bf16), pltpu.VMEM((rows, 4 * cols), f32)],
        2 * rows * width * 4 * cols,
        len(after),
        "forward",
        *blocks,
        *packs,
        *squares,
        *after,
    )
    return out[0], out[1:-1], out[-1]


def merge_y_kernel(left, *refs):
    pieces, (keep, send) = refs[:4], refs[-2:]
    for r in range(0, keep.shape[0], 32):
        at = pl.ds(r, 32)
        total = pieces[0][at, left : left + keep.shape[1]]
        for piece in pieces[1:]:
            total = total + piece[at, :].astype(f32)
        keep[at, :] = total
        send[at, :] = total.astype(bf16)


def merge_y(mine, got, left=0, after=()):
    return vmem_call(
        functools.partial(merge_y_kernel, left),
        [jax.ShapeDtypeStruct(got[0].shape, t) for t in (f32, bf16)],
        [],
        4 * mine.size,
        len(after),
        "merge_y",
        mine,
        *got,
        *after,
    )


def merge_x_kernel(parts, n_above, keep, got, *refs):
    outs = refs[-parts:]
    part = outs[0].shape[1]
    start = 0
    for above in refs[:n_above]:
        outs[0][: above.shape[0], :] = above[...]
        start = above.shape[0]
    for k, out in enumerate(outs):
        at = slice(k * part, (k + 1) * part)
        out[start:, :] = (keep[:, at] + got[:, at].astype(f32)).astype(bf16)


def merge_x(keep, got, parts, above=(), after=()):
    rows, width = keep.shape
    rows += sum(a.shape[0] for a in above)
    return vmem_call(
        functools.partial(merge_x_kernel, parts, len(above)),
        [jax.ShapeDtypeStruct((rows, width // parts), bf16)] * parts,
        [],
        keep.size,
        len(after),
        "merge_x",
        keep,
        got,
        *above,
        *after,
    )


def backward_kernel(n, scale, groups, more, *refs):
    blocks, targets, o_ref, held = refs[:n], refs[n : n + 4], refs[-2], refs[-1]
    y = place()[4]
    width = blocks[0].shape[1]
    for ref, dy in zip(targets, (0,) + AHEAD):
        count = ref.shape[0] // groups
        for g in range(groups):
            at = rows_at(4 * g + ((y - dy) & 3), count)
            held[at, :] = ref[g * count : (g + 1) * count, :]
    for at in range(0, width, 256):
        tokens = jnp.concatenate([block[:, at : at + 256] for block in blocks], axis=0)
        value = lax.dot_general(
            tokens, held[...], (((0,), (0,)), ((), ())), preferred_element_type=f32
        )
        value = value * scale
        if more:
            value = value + refs[n + 4][at : at + 256, :]
        o_ref[at : at + 256, :] = value.astype(o_ref.dtype)


def backward(blocks, targets, dtype, groups=1, init=(), after=()):
    n, width, cols = len(blocks), blocks[0].shape[1], targets[0].shape[1]
    rows = sum(block.shape[0] for block in blocks)
    return vmem_call(
        functools.partial(backward_kernel, n, 1.0 / math.sqrt(TOKENS), groups, len(init)),
        jax.ShapeDtypeStruct((width, cols), dtype),
        [pltpu.VMEM((rows, cols), bf16)],
        2 * rows * width * cols,
        len(after),
        "backward",
        *blocks,
        *targets,
        *init,
        *after,
    )


def gate_kernel(*refs):
    pass


def gate(value, *after):
    hbm = pl.BlockSpec(memory_space=pl.ANY)
    return pl.pallas_call(
        gate_kernel,
        out_shape=jax.ShapeDtypeStruct(value.shape, value.dtype),
        in_specs=[hbm] * (1 + len(after)),
        out_specs=hbm,
        input_output_aliases={0: 0},
        compiler_params=pltpu.CompilerParams(vmem_limit_bytes=1024 * 1024),
        cost_estimate=pl.CostEstimate(flops=0, bytes_accessed=0, transcendentals=0),
        name="gate",
    )(value, *after)


def body(hidden, residual, down_weight, mask, state):
    cols = down_weight.shape[1]
    keep = mask == 1

    def ring(value):
        return lax.ppermute(value, "dp", RING)

    def swap(value):
        return lax.ppermute(value, "dp", PAIR_CORE)

    def across(value):
        return lax.ppermute(value, "dp", PAIR_X)

    def around(pieces):
        ahead = AHEAD * (len(pieces) // 3)
        return [lax.ppermute(v, "mp", y_perm(dy)) for v, dy in zip(pieces, ahead)]

    def over(value):
        return lax.ppermute(value, "mp", PAIR_X_HI)

    sib = swap(hidden)
    a1 = ring(hidden)
    b1 = ring(sib)
    weight_x = across(down_weight)
    pruned = jnp.where(keep, jnp.zeros_like(down_weight), -down_weight)
    pruned_x = across(pruned)
    residual_x = across(residual)
    a1 = gate(a1, pruned)
    a2 = ring(a1)
    sa1 = swap(a1)
    b1 = gate(b1, weight_x)
    b2 = ring(b1)
    sb1 = swap(b1)
    a2 = gate(a2, sa1, sb1, pruned_x)
    a3 = ring(a2)
    sa2 = swap(a2)
    b3 = ring(b2)

    packs = (down_weight, pruned, weight_x, pruned_x, residual, residual_x)
    early = [[hidden, sib], [a1, b1], [sa1, sb1], [a2, sa2]]
    places = [(0, 1), (0, 0), (1, 1), (1, 0), (-1, 0), (-1, 1), (2, 1), (-2, 0)]
    mine0, ahead0, squares0 = forward(early, places, packs, 1)
    got0 = around(ahead0)
    a3 = gate(a3, squares0)
    a4 = ring(a3)
    keep0, send0 = merge_y(mine0, got0)
    b3 = gate(b3, keep0)
    s4 = stack([b2, a3, b3, a4])
    t4 = swap(s4)
    late = [s4, t4]
    places = [(2, 0), (3, 1), (3, 0), (4, 1), (-2, 1), (-3, 0), (-3, 1), (4, 0)]
    mine1, ahead1, squares = forward([[s4], [t4]], places, packs, 2, [squares0], [keep0])
    squares_x = across(squares)

    early = [block for unit in early for block in unit]
    sent0 = over(send0)
    own0, other0 = merge_x(keep0, sent0, 2, (), [squares])
    keep1, send1 = merge_y(mine1, around(ahead1[3:]), 2 * cols, [other0])
    back0 = around([other0] * 3)
    (other1,) = merge_x(keep1, over(send1), 1, (), back0[:1])
    init = backward(early, [other0] + back0, f32)
    back1 = around([other1] * 3)
    got2 = around([gate(v, keep1) for v in ahead1[:3]])
    keep2, send2 = merge_y(mine1, got2, 0, [squares_x])
    sent2 = over(send2)
    arrived = across(backward(late, [other1] + back1, bf16, 1, [init], [sent2]))
    (own,) = merge_x(keep2, sent2, 1, [own0])
    grads = backward(early + late, [own] + around([own] * 3), f32, 2)
    colsq = squares + squares_x
    grads = grads + arrived.astype(f32)

    grad_out = grads[:, :cols]
    grad_step = jnp.where(keep, grads[:, cols:], jnp.float32(0.0))
    rms = jnp.sqrt(colsq.reshape(-1) / TOKENS + 1e-05)
    weight_f = down_weight.astype(f32)
    scores = jnp.abs(weight_f) * (score_alpha * jnp.abs(grad_out) + rms[:, None])
    new_state = decay_rate * state + (1.0 - decay_rate) * grad_step * grad_step
    moved = weight_f - step_rate * grad_step / (jnp.sqrt(new_state) + tiny_eps)
    new_weight = jnp.where(keep, moved, jnp.float32(0.0)).astype(bf16)
    return (scores, new_weight, new_state)


def solution(mesh):
    return jax.shard_map(
        body,
        mesh=mesh,
        in_specs=(P("dp", "mp"), P("mp", "dp"), P("mp", "dp"), P("mp", "dp"), P("mp", "dp")),
        out_specs=(P("mp", "dp"), P("mp", "dp"), P("mp", "dp")),
        check_vma=False,
    )
```

```python
import functools
import math

import jax
import jax.numpy as jnp
from jax import lax
from jax.experimental import pallas as pl
from jax.experimental.pallas import tpu as pltpu
from jax.sharding import PartitionSpec as P

FFW = 14336
TOKENS = 4096

score_alpha = 0.5
decay_rate = 0.9
step_rate = 0.3
tiny_eps = 1e-08

Z = 8
MP = 8
PAIR_CORE = [(i, i ^ 1) for i in range(32)]
PAIR_X = [(i, i ^ 16) for i in range(32)]
VMEM_LIMIT = 16 * 1024 * 1024

f32, bf16 = jnp.float32, jnp.bfloat16


def ring_perm():
    out = []
    for i in range(32):
        x, z, c = i // 16, (i // 2) % Z, i % 2
        z = (z + (1 if c == 0 else -1)) % Z
        out.append((i, x * 16 + z * 2 + c))
    return out


RING = ring_perm()


def y_perm(dy):
    return [(j, (j // 4) * 4 + (j % 4 + dy) % 4) for j in range(MP)]


PAIR_X_HI = [(j, j ^ 4) for j in range(MP)]
AHEAD = (1, 3, 2)


def place():
    dp, mp = lax.axis_index("dp"), lax.axis_index("mp")
    return dp >> 4, (dp >> 1) & 7, dp & 1, mp >> 2, mp & 3


def rows_at(block, count):
    return pl.ds(pl.multiple_of(block * count, 32), count)


def vmem_call(kernel, out_shape, scratch, flops, n_after, name, *args):
    vmem = pl.BlockSpec(memory_space=pltpu.VMEM)
    specs = [vmem] * (len(args) - n_after)
    specs += [pl.BlockSpec(memory_space=pl.ANY)] * n_after
    moved = sum(a.size * a.dtype.itemsize for a in args)
    return pl.pallas_call(
        kernel,
        out_shape=out_shape,
        in_specs=specs,
        out_specs=jax.tree.map(lambda _: vmem, out_shape),
        scratch_shapes=scratch,
        compiler_params=pltpu.CompilerParams(vmem_limit_bytes=VMEM_LIMIT),
        cost_estimate=pl.CostEstimate(flops=0, bytes_accessed=0, transcendentals=0),
        name=name,
    )(*args)


def stack_kernel(n, *refs):
    rows = refs[0].shape[0]
    for k in range(n):
        refs[-1][k * rows : (k + 1) * rows, :] = refs[k][...]


def stack(blocks, after=()):
    rows, width = blocks[0].shape
    return vmem_call(
        functools.partial(stack_kernel, len(blocks)),
        jax.ShapeDtypeStruct((len(blocks) * rows, width), bf16),
        [],
        0,
        len(after),
        "stack",
        *blocks,
        *after,
    )


ROWS = 128


def forward_kernel(units, places, scale, more, sides, *refs):
    blocks = refs[: sum(units)]
    packs, residuals = refs[sum(units) :][:4], refs[sum(units) + 4 :][:2]
    mine, ahead = refs[-4 - 3 * sides], refs[-3 - 3 * sides : -3]
    sq_ref, wide, held = refs[-3:]
    x, z, c, x_hi, y = place()
    back = 2 * c - 1
    width, cols = blocks[0].shape[1], packs[0].shape[1]
    for k, ref in enumerate(packs):
        wide[:, k * cols : (k + 1) * cols] = ref[...]
    total = jnp.zeros((8, width), f32)
    first, row = 0, 0
    for unit in units:
        group = [block[...] for block in blocks[first : first + unit]]
        tokens = jnp.concatenate(group, axis=0) if unit > 1 else group[0]
        first += unit
        for side, ref in enumerate(residuals):
            left = side * 2 * cols
            weights = wide[:, left : left + 2 * cols]
            value = jnp.dot(tokens, weights, preferred_element_type=f32) * scale
            for k in range(tokens.shape[0] // ROWS):
                step, same = places[row // ROWS + k]
                at = (z + step * back) & 7
                core = c if same else 1 - c
                here = (x_hi << 2) + y == (x << 2) + (at >> 1)
                start = pl.multiple_of(((at & 1) << 8) + (core << 7), ROWS)
                extra = jnp.where(here, ref[pl.ds(start, ROWS), :].astype(f32), 0.0)
                part = value[k * ROWS : (k + 1) * ROWS]
                to = pl.ds(row + k * ROWS, ROWS)
                held[to, left : left + cols] = part[:, :cols] + extra
                held[to, left + cols : left + 2 * cols] = part[:, cols:]
        squares = jnp.square(tokens.astype(f32))
        total = total + jnp.sum(squares.reshape(-1, 8, width), axis=0)
        row += tokens.shape[0]
    total = jnp.sum(total, axis=0, keepdims=True)
    sq_ref[...] = total + refs[sum(units) + 6][...] if more else total
    quarter = held.shape[0] // 4
    mine[...] = held[rows_at(y, quarter), :]
    part = held.shape[1] // sides
    for k, out in enumerate(ahead):
        at = rows_at((y + AHEAD[k % 3]) & 3, quarter)
        left = (k // 3) * part
        out[...] = held[at, left : left + part].astype(bf16)


def forward(units, places, packs, sides, squares=(), after=()):
    blocks = [block for unit in units for block in unit]
    rows = sum(block.shape[0] for block in blocks)
    width, cols = blocks[0].shape[1], packs[0].shape[1]
    piece = (rows // 4, 4 * cols)
    out = vmem_call(
        functools.partial(
            forward_kernel,
            [len(unit) for unit in units],
            places,
            1.0 / math.sqrt(FFW),
            len(squares),
            sides,
        ),
        [jax.ShapeDtypeStruct(piece, f32)]
        + [jax.ShapeDtypeStruct((rows // 4, 4 * cols // sides), bf16)] * (3 * sides)
        + [jax.ShapeDtypeStruct((1, width), f32)],
        [pltpu.VMEM((width, 4 * cols), bf16), pltpu.VMEM((rows, 4 * cols), f32)],
        2 * rows * width * 4 * cols,
        len(after),
        "forward",
        *blocks,
        *packs,
        *squares,
        *after,
    )
    return out[0], out[1:-1], out[-1]


def merge_y_kernel(left, *refs):
    pieces, (keep, send) = refs[:4], refs[-2:]
    for r in range(0, keep.shape[0], 32):
        at = pl.ds(r, 32)
        total = pieces[0][at, left : left + keep.shape[1]]
        for piece in pieces[1:]:
            total = total + piece[at, :].astype(f32)
        keep[at, :] = total
        send[at, :] = total.astype(bf16)


def merge_y(mine, got, left=0, after=()):
    return vmem_call(
        functools.partial(merge_y_kernel, left),
        [jax.ShapeDtypeStruct(got[0].shape, t) for t in (f32, bf16)],
        [],
        4 * mine.size,
        len(after),
        "merge_y",
        mine,
        *got,
        *after,
    )


def merge_x_kernel(parts, n_above, keep, got, *refs):
    outs = refs[-parts:]
    part = outs[0].shape[1]
    start = 0
    for above in refs[:n_above]:
        outs[0][: above.shape[0], :] = above[...]
        start = above.shape[0]
    for k, out in enumerate(outs):
        at = slice(k * part, (k + 1) * part)
        out[start:, :] = (keep[:, at] + got[:, at].astype(f32)).astype(bf16)


def merge_x(keep, got, parts, above=(), after=()):
    rows, width = keep.shape
    rows += sum(a.shape[0] for a in above)
    return vmem_call(
        functools.partial(merge_x_kernel, parts, len(above)),
        [jax.ShapeDtypeStruct((rows, width // parts), bf16)] * parts,
        [],
        keep.size,
        len(after),
        "merge_x",
        keep,
        got,
        *above,
        *after,
    )


def backward_kernel(n, scale, groups, more, *refs):
    blocks, targets, o_ref, held = refs[:n], refs[n : n + 4], refs[-2], refs[-1]
    y = place()[4]
    width = blocks[0].shape[1]
    for ref, dy in zip(targets, (0,) + AHEAD):
        count = ref.shape[0] // groups
        for g in range(groups):
            at = rows_at(4 * g + ((y - dy) & 3), count)
            held[at, :] = ref[g * count : (g + 1) * count, :]
    for at in range(0, width, 256):
        tokens = jnp.concatenate([block[:, at : at + 256] for block in blocks], axis=0)
        value = lax.dot_general(
            tokens, held[...], (((0,), (0,)), ((), ())), preferred_element_type=f32
        )
        value = value * scale
        if more:
            value = value + refs[n + 4][at : at + 256, :]
        o_ref[at : at + 256, :] = value.astype(o_ref.dtype)


def backward(blocks, targets, dtype, groups=1, init=(), after=()):
    n, width, cols = len(blocks), blocks[0].shape[1], targets[0].shape[1]
    rows = sum(block.shape[0] for block in blocks)
    return vmem_call(
        functools.partial(backward_kernel, n, 1.0 / math.sqrt(TOKENS), groups, len(init)),
        jax.ShapeDtypeStruct((width, cols), dtype),
        [pltpu.VMEM((rows, cols), bf16)],
        2 * rows * width * cols,
        len(after),
        "backward",
        *blocks,
        *targets,
        *init,
        *after,
    )


def gate_kernel(*refs):
    pass


def gate(value, *after):
    hbm = pl.BlockSpec(memory_space=pl.ANY)
    return pl.pallas_call(
        gate_kernel,
        out_shape=jax.ShapeDtypeStruct(value.shape, value.dtype),
        in_specs=[hbm] * (1 + len(after)),
        out_specs=hbm,
        input_output_aliases={0: 0},
        compiler_params=pltpu.CompilerParams(vmem_limit_bytes=1024 * 1024),
        cost_estimate=pl.CostEstimate(flops=0, bytes_accessed=0, transcendentals=0),
        name="gate",
    )(value, *after)


def body(hidden, residual, down_weight, mask, state):
    cols = down_weight.shape[1]
    keep = mask == 1

    def ring(value):
        return lax.ppermute(value, "dp", RING)

    def swap(value):
        return lax.ppermute(value, "dp", PAIR_CORE)

    def across(value):
        return lax.ppermute(value, "dp", PAIR_X)

    def around(pieces):
        ahead = AHEAD * (len(pieces) // 3)
        return [lax.ppermute(v, "mp", y_perm(dy)) for v, dy in zip(pieces, ahead)]

    def over(value):
        return lax.ppermute(value, "mp", PAIR_X_HI)

    sib = swap(hidden)
    a1 = ring(hidden)
    b1 = ring(sib)
    weight_x = across(down_weight)
    pruned = jnp.where(keep, jnp.zeros_like(down_weight), -down_weight)
    pruned_x = across(pruned)
    residual_x = across(residual)
    a1 = gate(a1, pruned)
    a2 = ring(a1)
    sa1 = swap(a1)
    b1 = gate(b1, weight_x)
    b2 = ring(b1)
    sb1 = swap(b1)
    a2 = gate(a2, sa1, sb1, pruned_x)
    a3 = ring(a2)
    sa2 = swap(a2)
    b3 = ring(b2)

    packs = (down_weight, pruned, weight_x, pruned_x, residual, residual_x)
    early = [[hidden, sib], [a1, b1], [sa1, sb1], [a2, sa2]]
    places = [(0, 1), (0, 0), (1, 1), (1, 0), (-1, 0), (-1, 1), (2, 1), (-2, 0)]
    mine0, ahead0, squares0 = forward(early, places, packs, 1)
    got0 = around(ahead0)
    a3 = gate(a3, squares0)
    a4 = ring(a3)
    keep0, send0 = merge_y(mine0, got0)
    b3 = gate(b3, keep0)
    s4 = stack([b2, a3, b3, a4])
    t4 = swap(s4)
    late = [s4, t4]
    places = [(2, 0), (3, 1), (3, 0), (4, 1), (-2, 1), (-3, 0), (-3, 1), (4, 0)]
    mine1, ahead1, squares = forward([[s4], [t4]], places, packs, 2, [squares0], [keep0])
    squares_x = across(squares)

    early = [block for unit in early for block in unit]
    sent0 = over(send0)
    own0, other0 = merge_x(keep0, sent0, 2, (), [squares])
    keep1, send1 = merge_y(mine1, around(ahead1[3:]), 2 * cols, [other0])
    back0 = around([other0] * 3)
    (other1,) = merge_x(keep1, over(send1), 1, (), back0)
    init = backward(early, [other0] + back0, f32)
    back1 = around([other1] * 3)
    got2 = around([gate(v, keep1) for v in ahead1[:3]])
    keep2, send2 = merge_y(mine1, got2, 0, [squares_x])
    sent2 = over(send2)
    arrived = across(backward(late, [other1] + back1, bf16, 1, [init], [sent2]))
    (own,) = merge_x(keep2, sent2, 1, [own0])
    grads = backward(early + late, [own] + around([own] * 3), f32, 2)
    colsq = squares + squares_x
    grads = grads + arrived.astype(f32)

    grad_out = grads[:, :cols]
    grad_step = jnp.where(keep, grads[:, cols:], jnp.float32(0.0))
    rms = jnp.sqrt(colsq.reshape(-1) / TOKENS + 1e-05)
    weight_f = down_weight.astype(f32)
    scores = jnp.abs(weight_f) * (score_alpha * jnp.abs(grad_out) + rms[:, None])
    new_state = decay_rate * state + (1.0 - decay_rate) * grad_step * grad_step
    moved = weight_f - step_rate * grad_step / (jnp.sqrt(new_state) + tiny_eps)
    new_weight = jnp.where(keep, moved, jnp.float32(0.0)).astype(bf16)
    return (scores, new_weight, new_state)


def solution(mesh):
    return jax.shard_map(
        body,
        mesh=mesh,
        in_specs=(P("dp", "mp"), P("mp", "dp"), P("mp", "dp"), P("mp", "dp"), P("mp", "dp")),
        out_specs=(P("mp", "dp"), P("mp", "dp"), P("mp", "dp")),
        check_vma=False,
    )
```

```python
import functools
import math

import jax
import jax.numpy as jnp
from jax import lax
from jax.experimental import pallas as pl
from jax.experimental.pallas import tpu as pltpu
from jax.sharding import PartitionSpec as P

FFW = 14336
TOKENS = 4096

score_alpha = 0.5
decay_rate = 0.9
step_rate = 0.3
tiny_eps = 1e-08

Z = 8
MP = 8
PAIR_CORE = [(i, i ^ 1) for i in range(32)]
PAIR_X = [(i, i ^ 16) for i in range(32)]
VMEM_LIMIT = 16 * 1024 * 1024

f32, bf16 = jnp.float32, jnp.bfloat16


def ring_perm():
    out = []
    for i in range(32):
        x, z, c = i // 16, (i // 2) % Z, i % 2
        z = (z + (1 if c == 0 else -1)) % Z
        out.append((i, x * 16 + z * 2 + c))
    return out


RING = ring_perm()


def y_perm(dy):
    return [(j, (j // 4) * 4 + (j % 4 + dy) % 4) for j in range(MP)]


PAIR_X_HI = [(j, j ^ 4) for j in range(MP)]
AHEAD = (1, 3, 2)


def place():
    dp, mp = lax.axis_index("dp"), lax.axis_index("mp")
    return dp >> 4, (dp >> 1) & 7, dp & 1, mp >> 2, mp & 3


def rows_at(block, count):
    return pl.ds(pl.multiple_of(block * count, 32), count)


def vmem_call(kernel, out_shape, scratch, flops, n_after, name, *args):
    vmem = pl.BlockSpec(memory_space=pltpu.VMEM)
    specs = [vmem] * (len(args) - n_after)
    specs += [pl.BlockSpec(memory_space=pl.ANY)] * n_after
    moved = sum(a.size * a.dtype.itemsize for a in args)
    return pl.pallas_call(
        kernel,
        out_shape=out_shape,
        in_specs=specs,
        out_specs=jax.tree.map(lambda _: vmem, out_shape),
        scratch_shapes=scratch,
        compiler_params=pltpu.CompilerParams(vmem_limit_bytes=VMEM_LIMIT),
        cost_estimate=pl.CostEstimate(flops=0, bytes_accessed=0, transcendentals=0),
        name=name,
    )(*args)


def stack_kernel(n, *refs):
    rows = refs[0].shape[0]
    for k in range(n):
        refs[-1][k * rows : (k + 1) * rows, :] = refs[k][...]


def stack(blocks, after=()):
    rows, width = blocks[0].shape
    return vmem_call(
        functools.partial(stack_kernel, len(blocks)),
        jax.ShapeDtypeStruct((len(blocks) * rows, width), bf16),
        [],
        0,
        len(after),
        "stack",
        *blocks,
        *after,
    )


ROWS = 128


def forward_kernel(units, places, scale, more, sides, *refs):
    blocks = refs[: sum(units)]
    packs, residuals = refs[sum(units) :][:4], refs[sum(units) + 4 :][:2]
    mine, ahead = refs[-4 - 3 * sides], refs[-3 - 3 * sides : -3]
    sq_ref, wide, held = refs[-3:]
    x, z, c, x_hi, y = place()
    back = 2 * c - 1
    width, cols = blocks[0].shape[1], packs[0].shape[1]
    for k, ref in enumerate(packs):
        wide[:, k * cols : (k + 1) * cols] = ref[...]
    total = jnp.zeros((8, width), f32)
    first, row = 0, 0
    for unit in units:
        group = [block[...] for block in blocks[first : first + unit]]
        tokens = jnp.concatenate(group, axis=0) if unit > 1 else group[0]
        first += unit
        for side, ref in enumerate(residuals):
            left = side * 2 * cols
            weights = wide[:, left : left + 2 * cols]
            value = jnp.dot(tokens, weights, preferred_element_type=f32) * scale
            for k in range(tokens.shape[0] // ROWS):
                step, same = places[row // ROWS + k]
                at = (z + step * back) & 7
                core = c if same else 1 - c
                here = (x_hi << 2) + y == (x << 2) + (at >> 1)
                start = pl.multiple_of(((at & 1) << 8) + (core << 7), ROWS)
                extra = jnp.where(here, ref[pl.ds(start, ROWS), :].astype(f32), 0.0)
                part = value[k * ROWS : (k + 1) * ROWS]
                to = pl.ds(row + k * ROWS, ROWS)
                held[to, left : left + cols] = part[:, :cols] + extra
                held[to, left + cols : left + 2 * cols] = part[:, cols:]
        squares = jnp.square(tokens.astype(f32))
        total = total + jnp.sum(squares.reshape(-1, 8, width), axis=0)
        row += tokens.shape[0]
    total = jnp.sum(total, axis=0, keepdims=True)
    sq_ref[...] = total + refs[sum(units) + 6][...] if more else total
    quarter = held.shape[0] // 4
    mine[...] = held[rows_at(y, quarter), :]
    part = held.shape[1] // sides
    for k, out in enumerate(ahead):
        at = rows_at((y + AHEAD[k % 3]) & 3, quarter)
        left = (k // 3) * part
        out[...] = held[at, left : left + part].astype(bf16)


def forward(units, places, packs, sides, squares=(), after=()):
    blocks = [block for unit in units for block in unit]
    rows = sum(block.shape[0] for block in blocks)
    width, cols = blocks[0].shape[1], packs[0].shape[1]
    piece = (rows // 4, 4 * cols)
    out = vmem_call(
        functools.partial(
            forward_kernel,
            [len(unit) for unit in units],
            places,
            1.0 / math.sqrt(FFW),
            len(squares),
            sides,
        ),
        [jax.ShapeDtypeStruct(piece, f32)]
        + [jax.ShapeDtypeStruct((rows // 4, 4 * cols // sides), bf16)] * (3 * sides)
        + [jax.ShapeDtypeStruct((1, width), f32)],
        [pltpu.VMEM((width, 4 * cols), bf16), pltpu.VMEM((rows, 4 * cols), f32)],
        2 * rows * width * 4 * cols,
        len(after),
        "forward",
        *blocks,
        *packs,
        *squares,
        *after,
    )
    return out[0], out[1:-1], out[-1]


def merge_y_kernel(left, *refs):
    pieces, (keep, send) = refs[:4], refs[-2:]
    for r in range(0, keep.shape[0], 32):
        at = pl.ds(r, 32)
        total = pieces[0][at, left : left + keep.shape[1]]
        for piece in pieces[1:]:
            total = total + piece[at, :].astype(f32)
        keep[at, :] = total
        send[at, :] = total.astype(bf16)


def merge_y(mine, got, left=0, after=()):
    return vmem_call(
        functools.partial(merge_y_kernel, left),
        [jax.ShapeDtypeStruct(got[0].shape, t) for t in (f32, bf16)],
        [],
        4 * mine.size,
        len(after),
        "merge_y",
        mine,
        *got,
        *after,
    )


def merge_x_kernel(parts, n_above, keep, got, *refs):
    outs = refs[-parts:]
    part = outs[0].shape[1]
    start = 0
    for above in refs[:n_above]:
        outs[0][: above.shape[0], :] = above[...]
        start = above.shape[0]
    for k, out in enumerate(outs):
        at = slice(k * part, (k + 1) * part)
        out[start:, :] = (keep[:, at] + got[:, at].astype(f32)).astype(bf16)


def merge_x(keep, got, parts, above=(), after=()):
    rows, width = keep.shape
    rows += sum(a.shape[0] for a in above)
    return vmem_call(
        functools.partial(merge_x_kernel, parts, len(above)),
        [jax.ShapeDtypeStruct((rows, width // parts), bf16)] * parts,
        [],
        keep.size,
        len(after),
        "merge_x",
        keep,
        got,
        *above,
        *after,
    )


def backward_kernel(n, scale, groups, more, *refs):
    blocks, targets, o_ref, held = refs[:n], refs[n : n + 4], refs[-2], refs[-1]
    y = place()[4]
    width = blocks[0].shape[1]
    for ref, dy in zip(targets, (0,) + AHEAD):
        count = ref.shape[0] // groups
        for g in range(groups):
            at = rows_at(4 * g + ((y - dy) & 3), count)
            held[at, :] = ref[g * count : (g + 1) * count, :]
    for at in range(0, width, 256):
        tokens = jnp.concatenate([block[:, at : at + 256] for block in blocks], axis=0)
        value = lax.dot_general(
            tokens, held[...], (((0,), (0,)), ((), ())), preferred_element_type=f32
        )
        value = value * scale
        if more:
            value = value + refs[n + 4][at : at + 256, :]
        o_ref[at : at + 256, :] = value.astype(o_ref.dtype)


def backward(blocks, targets, dtype, groups=1, init=(), after=()):
    n, width, cols = len(blocks), blocks[0].shape[1], targets[0].shape[1]
    rows = sum(block.shape[0] for block in blocks)
    return vmem_call(
        functools.partial(backward_kernel, n, 1.0 / math.sqrt(TOKENS), groups, len(init)),
        jax.ShapeDtypeStruct((width, cols), dtype),
        [pltpu.VMEM((rows, cols), bf16)],
        2 * rows * width * cols,
        len(after),
        "backward",
        *blocks,
        *targets,
        *init,
        *after,
    )


def gate_kernel(*refs):
    pass


def gate(value, *after):
    hbm = pl.BlockSpec(memory_space=pl.ANY)
    return pl.pallas_call(
        gate_kernel,
        out_shape=jax.ShapeDtypeStruct(value.shape, value.dtype),
        in_specs=[hbm] * (1 + len(after)),
        out_specs=hbm,
        input_output_aliases={0: 0},
        compiler_params=pltpu.CompilerParams(vmem_limit_bytes=1024 * 1024),
        cost_estimate=pl.CostEstimate(flops=0, bytes_accessed=0, transcendentals=0),
        name="gate",
    )(value, *after)


def body(hidden, residual, down_weight, mask, state):
    cols = down_weight.shape[1]
    keep = mask == 1

    def ring(value):
        return lax.ppermute(value, "dp", RING)

    def swap(value):
        return lax.ppermute(value, "dp", PAIR_CORE)

    def across(value):
        return lax.ppermute(value, "dp", PAIR_X)

    def around(pieces):
        ahead = AHEAD * (len(pieces) // 3)
        return [lax.ppermute(v, "mp", y_perm(dy)) for v, dy in zip(pieces, ahead)]

    def over(value):
        return lax.ppermute(value, "mp", PAIR_X_HI)

    sib = swap(hidden)
    a1 = ring(hidden)
    b1 = ring(sib)
    weight_x = across(down_weight)
    pruned = jnp.where(keep, jnp.zeros_like(down_weight), -down_weight)
    pruned_x = across(pruned)
    residual_x = across(residual)
    a1 = gate(a1, pruned)
    a2 = ring(a1)
    sa1 = swap(a1)
    b1 = gate(b1, weight_x)
    b2 = ring(b1)
    sb1 = swap(b1)
    a2 = gate(a2, sa1, sb1, pruned_x)
    a3 = ring(a2)
    sa2 = swap(a2)
    b3 = ring(b2)

    packs = (down_weight, pruned, weight_x, pruned_x, residual, residual_x)
    early = [[hidden, sib], [a1, b1], [sa1, sb1], [a2, sa2]]
    places = [(0, 1), (0, 0), (1, 1), (1, 0), (-1, 0), (-1, 1), (2, 1), (-2, 0)]
    mine0, ahead0, squares0 = forward(early, places, packs, 1)
    got0 = around(ahead0)
    a3 = gate(a3, squares0)
    a4 = ring(a3)
    keep0, send0 = merge_y(mine0, got0)
    b3 = gate(b3, keep0)
    s4 = stack([b2, a3, b3, a4])
    t4 = swap(s4)
    late = [s4, t4]
    places = [(2, 0), (3, 1), (3, 0), (4, 1), (-2, 1), (-3, 0), (-3, 1), (4, 0)]
    mine1, ahead1, squares = forward([[s4], [t4]], places, packs, 2, [squares0], [keep0])
    squares_x = across(squares)

    early = [block for unit in early for block in unit]
    sent0 = over(send0)
    own0, other0 = merge_x(keep0, sent0, 2, (), [squares])
    keep1, send1 = merge_y(mine1, around(ahead1[3:]), 2 * cols, [other0])
    back0 = around([other0] * 3)
    (other1,) = merge_x(keep1, over(send1), 1, (), back0)
    init = backward(early, [other0] + back0, f32)
    back1 = around([other1] * 3)
    got2 = around([gate(v, keep1) for v in ahead1[:3]])
    keep2, send2 = merge_y(mine1, got2)
    sent2 = over(send2)
    arrived = across(backward(late, [other1] + back1, bf16, 1, [init], [sent2, squares_x]))
    (own,) = merge_x(keep2, sent2, 1, [own0])
    grads = backward(early + late, [own] + around([own] * 3), f32, 2)
    colsq = squares + squares_x
    grads = grads + arrived.astype(f32)

    grad_out = grads[:, :cols]
    grad_step = jnp.where(keep, grads[:, cols:], jnp.float32(0.0))
    rms = jnp.sqrt(colsq.reshape(-1) / TOKENS + 1e-05)
    weight_f = down_weight.astype(f32)
    scores = jnp.abs(weight_f) * (score_alpha * jnp.abs(grad_out) + rms[:, None])
    new_state = decay_rate * state + (1.0 - decay_rate) * grad_step * grad_step
    moved = weight_f - step_rate * grad_step / (jnp.sqrt(new_state) + tiny_eps)
    new_weight = jnp.where(keep, moved, jnp.float32(0.0)).astype(bf16)
    return (scores, new_weight, new_state)


def solution(mesh):
    return jax.shard_map(
        body,
        mesh=mesh,
        in_specs=(P("dp", "mp"), P("mp", "dp"), P("mp", "dp"), P("mp", "dp"), P("mp", "dp")),
        out_specs=(P("mp", "dp"), P("mp", "dp"), P("mp", "dp")),
        check_vma=False,
    )
```
